256 devices in a mesh: blk: 64 (over y, z, x_lo), rep: 4 (over x_hi, core).
Axes of the slice: x: 4 (x_hi: 2, x_lo: 2; x = x_hi * 2 + x_lo), y: 4, z: 8, core: 2. Of those that a mesh axis runs over, the one named last changes fastest.
Arguments:
- layer_input: bfloat16 [98304, 8192], P(('blk', 'rep')), may hold values from -24 to 24
- norm_gain: bfloat16 [8192], replicated, may hold values from 0.099609375 to 1.8984375
- key_cotangent: bfloat16 [98304, 512], P(('blk', 'rep')), may hold values from -6 to 6
- segment_ids: int32 [98304], P(('blk', 'rep')), may hold values from 0 to 2
- key_weight: bfloat16 [8192, 512], P('blk'), may hold values from -0.0625 to 0.0625
Outputs:
- weight_grad: float32 [8192, 512], P('blk')
- input_grad: bfloat16 [98304, 8192], P(('blk', 'rep'))
The draws below stay inside these ranges and needn't reach their ends.
All inputs are finite; a program needn't handle non-finite values.
Results may differ from the reference program's by a relative error of at most 0.0029.
Values may be sent and summed in bfloat16 or wider, within the bound.
A program may use at most 128 MiB of HBM per device.

```python
import jax
import jax.numpy as jnp
from jax import lax

D = 8192
TOK_DEV = 384
KW = 512
TOKENS = 98304
N_BLK = 64
N_REP = 4


def set_ends(values, own_key, smallest, top_value):
    index_at = [jax.random.randint(jax.random.fold_in(own_key, axis), (), 0, length) for axis, length in enumerate(values.shape)]
    widest = values.shape.index(max(values.shape))
    next_to = index_at[:widest] + [(index_at[widest] + 1) % values.shape[widest]] + index_at[widest + 1:]
    return values.at[tuple(index_at)].set(smallest).at[tuple(next_to)].set(top_value)


def strengthened(result, own_key, source, target, shards_of, factor):
    owner, partner = [(jnp.arange(result.shape[dim]) // (result.shape[dim] // shards_of)).reshape([-1 if axis == dim else 1 for axis in range(result.ndim)]) for dim in (source, target)]
    chosen = jax.random.permutation(own_key, shards_of)[partner]
    strong = (owner == chosen) | (owner == (partner + shards_of // 2) % shards_of)
    return jnp.where(strong, factor * result, result)


def block_levels(key, dims, split, least, top_value):
    level, own = 1.0, jax.random.fold_in(key, 6)
    for position, parts in split:
        heights = jnp.exp(jax.random.uniform(jax.random.fold_in(own, position), (parts,), jnp.float32, least / len(split), top_value / len(split)))
        level = level * jnp.repeat(heights, dims[position] // parts).reshape([-1 if axis == position else 1 for axis in range(len(dims))])
    return level


def scatter_about(own_key, extent, scale, reach, shards=(), dtype=jnp.bfloat16):
    result = jax.random.normal(own_key, extent, jnp.float32) * scale
    if len(shards) > 0:
        result = block_levels(own_key, extent, shards, -0.22, 0.18) * result
    return jnp.clip(result, min=-reach, max=reach).astype(dtype)


def noise_with(stream_key, shape, spread, bound, split, heavy, kind=jnp.bfloat16):
    array = spread * jax.random.normal(stream_key, shape, jnp.float32)
    if split:
        array = array * block_levels(stream_key, shape, split, -0.22, 0.18)
    return jnp.clip(strengthened(array, jax.random.fold_in(stream_key, 3), *heavy), -bound, bound).astype(kind)


def setup_inputs(seed: int = 0) -> dict:
    seeds = jax.random.split(jax.random.key(seed), 6)
    layer_input = noise_with(seeds[0], (TOKENS, D), 1.0, 24.0, ((0, 256),), (0, 1, 256, 6.0))
    norm_gain = jnp.clip(1.0 + 0.18 * jax.random.normal(seeds[1], (D,), jnp.float32), 0.099609375, 1.8984375).astype(jnp.bfloat16)
    key_cotangent = scatter_about(seeds[2], (TOKENS, KW), 1.0, 6.0, ((0, 256),))
    segment_ids = set_ends(jax.random.randint(seeds[3], (TOKENS,), 0, 3), jax.random.fold_in(seeds[3], 1), 0, 2).astype(jnp.int32)
    key_weight = scatter_about(seeds[4], (D, KW), D ** -0.5, 0.0625, ((0, 64),))
    return {"layer_input": layer_input, "norm_gain": norm_gain, "key_cotangent": key_cotangent, "segment_ids": segment_ids, "key_weight": key_weight}


def reference(layer_input, norm_gain, key_cotangent, segment_ids, key_weight):
    blocks = N_BLK * N_REP
    xb = layer_input.reshape(blocks, TOK_DEV, D)
    cb = key_cotangent.reshape(blocks, TOK_DEV, KW)
    sb = segment_ids.reshape(blocks, TOK_DEV)
    gain = norm_gain.astype(jnp.float32)

    def step(carry, item):
        xin, cin, sin = item
        xs = xin.astype(jnp.float32)
        rstd = 1.0 / jnp.sqrt(lax.optimization_barrier(jnp.mean(xs * xs, axis=1, keepdims=True)) + 1e-05)
        normed = (xs * rstd * gain).astype(jnp.bfloat16)
        live = jnp.where((sin != 0)[:, None], cin, jnp.zeros_like(cin))
        carry = carry + lax.dot_general(normed, live, (((0,), (0,)), ((), ())), preferred_element_type=jnp.float32)
        normed_grad = lax.dot_general(live, key_weight, (((1,), (1,)), ((), ())), preferred_element_type=jnp.float32)
        inner = lax.optimization_barrier(jnp.sum(xs * gain * normed_grad, axis=1, keepdims=True))
        xgrad = rstd * gain * normed_grad - xs * rstd ** 3 * inner / D
        return (carry, xgrad.astype(jnp.bfloat16))
    total, grads = lax.scan(step, jnp.zeros((D, KW), jnp.float32), (xb, cb, sb))
    weight_grad = total / jnp.sqrt(jnp.float32(TOKENS))
    return (weight_grad, grads.reshape(TOKENS, D))
```

```python
import jax
import jax.numpy as jnp
from jax import lax
from jax.experimental import pallas as pl
from jax.experimental.pallas import tpu as pltpu
from jax.sharding import PartitionSpec as P

F32 = jnp.float32
BF16 = jnp.bfloat16
NX, NY, NZ = 4, 4, 8
TOK, D, KW, TOKENS = 384, 8192, 512, 98304
CH = 256
NCH = D // CH


def dev(x, y, z, c):
    return {"blk": (y * NZ + z) * 2 + x % 2, "rep": (x // 2) * 2 + c}


class Ring:
    def __init__(self, own, subs, plus, minus, send, recv, ssem, rsem):
        self.own, self.subs, self.to = own, subs, (plus, minus)
        self.send, self.recv, self.ssem, self.rsem = send, recv, ssem, rsem

    def copy(self, i):
        return pltpu.make_async_remote_copy(
            self.send.at[i], self.recv.at[i], self.ssem.at[i], self.rsem.at[i], device_id=self.to[i % 2]
        )

    def put(self, i, rel, h, plus=None):
        for s in range(self.subs):
            v = self.own(rel, h, s)
            if plus is not None:
                v = v + self.recv[plus, s].astype(F32)
            self.send[i, s] = v.astype(self.send.dtype)
        self.copy(i).start()

    def far(self, h):
        self.put(h, 2, h)

    def single(self, d):
        self.put(2 + d, (1, 3)[d], (1, 0)[d])

    def combine(self, d):
        self.copy(d).wait_recv()
        self.put(4 + d, (1, 3)[d], d, plus=d)

    def mine_wait(self, h):
        for i in ((4, 3), (2, 5))[h]:
            self.copy(i).wait_recv()

    def mine(self, h, s):
        a, b = ((4, 3), (2, 5))[h]
        return self.own(0, h, s) + self.recv[a, s].astype(F32) + self.recv[b, s].astype(F32)

    def finish(self):
        for i in range(6):
            self.copy(i).wait_send()


def kernel(
    x_hbm, gain_ref, live_ref, w_hbm, wg_ref, ig_hbm,
    X, Wf, Nh, Ns, LT, S, NG, ACC, RB, A2, B2, T, Tb, ZR, O,
    r1x_s, r1x_r, r1y_s, r1y_r, r2y_s, r2y_r, r2x_s, r2x_r,
    xsem, wsem, osem, nss, nsr, lts, ltr,
    axs, axr, ays, ayr, zs, zr, shs, shr, sys_, syr,
    q1xs, q1xr, q1ys, q1yr, q2ys, q2yr, q2xs, q2xr,
    zds, zdr, fs, fr,
):
    b, r = lax.axis_index("blk"), lax.axis_index("rep")
    xl, z, y = b % 2, (b // 2) % NZ, b // (2 * NZ)
    xh, c = r // 2, r % 2
    x = 2 * xh + xl
    sib = dev(x, y, z, 1 - c)
    xp, xm = dev((x + 1) % 4, y, z, c), dev((x + 3) % 4, y, z, c)
    yp, ym = dev(x, (y + 1) % 4, z, c), dev(x, (y + 3) % 4, z, c)
    zp, zm = dev(x, y, (z + 1) % 8, c), dev(x, y, (z + 7) % 8, c)
    far_same, far_other = dev((x + 2) % 4, y, z, c), dev((x + 2) % 4, y, z, 1 - c)

    wcp = pltpu.make_async_copy(w_hbm, Wf.at[y, z, xl], wsem)
    wcp.start()

    def xcopy(j):
        return pltpu.make_async_copy(x_hbm.at[:, pl.ds(pl.multiple_of(j * CH, CH), CH)], X.at[j], xsem.at[j])

    lax.fori_loop(0, NCH, lambda j, u: (xcopy(j).start(), u)[1], 0)

    bar = pltpu.get_barrier_semaphore()
    met = [sib, xp, xm, yp, ym, far_same, far_other] + [dev(x, y, (z + k) % 8, c) for k in range(1, 8)]
    for d in met:
        pl.semaphore_signal(bar, 1, device_id=d)
    pl.semaphore_wait(bar, len(met))

    full, h0, h1 = pl.ds(64 * c, 64), pl.ds(64 * c, 32), pl.ds(64 * c + 32, 32)
    sfull, sh0, sh1 = pl.ds(64 - 64 * c, 64), pl.ds(64 - 64 * c, 32), pl.ds(96 - 64 * c, 32)
    col_y = (y, y, (y + 3) % 4, (y + 1) % 4, (y + 2) % 4)

    def region(col, zz, rows):
        if col == 0:
            return Wf.at[y, zz, xl, rows]
        if col == 1:
            return Wf.at[y, zz, 1 - xl, rows]
        return Wf.at[col_y[col], zz, :, rows]

    def rcopy(src, dst, ss, rs, to):
        return pltpu.make_async_remote_copy(src, dst, ss, rs, device_id=to)

    def same(ref, ss, rs, to):
        return rcopy(ref, ref, ss, rs, to)

    ax_out = [same(Wf.at[y, z, xl, h0], axs.at[0], axr.at[0], xp), same(Wf.at[y, z, xl, h1], axs.at[1], axr.at[1], xm)]
    ax_in = [
        rcopy(Wf.at[y, z, 1 - xl, h0], Wf.at[y, z, 1 - xl, h0], axs.at[0], axr.at[0], xp),
        rcopy(Wf.at[y, z, 1 - xl, h1], Wf.at[y, z, 1 - xl, h1], axs.at[1], axr.at[1], xm),
    ]
    own_pair = Wf.at[y, z, :, full]
    ay_out = [
        same(own_pair, ays.at[0], ayr.at[0], yp),
        same(own_pair, ays.at[1], ayr.at[1], ym),
        same(Wf.at[(y + 3) % 4, z, :, h0], ays.at[2], ayr.at[2], yp),
        same(Wf.at[(y + 1) % 4, z, :, h1], ays.at[3], ayr.at[3], ym),
    ]
    ay_in = [
        same(Wf.at[(y + 3) % 4, z, :, full], ays.at[0], ayr.at[0], yp),
        same(Wf.at[(y + 1) % 4, z, :, full], ays.at[1], ayr.at[1], ym),
        same(Wf.at[(y + 2) % 4, z, :, h0], ays.at[2], ayr.at[2], yp),
        same(Wf.at[(y + 2) % 4, z, :, h1], ays.at[3], ayr.at[3], ym),
    ]

    def z_at(d, k):
        return (z + 8 - k) % 8 if d == 0 else (z + k) % 8

    def z_out(col, d, k):
        rows = full if k < 4 else (h0, h1)[d]
        return same(region(col, z_at(d, k - 1), rows), zs.at[col, d, k - 1], zr.at[col, d, k - 1], (zp, zm)[d])

    def z_in(col, d, k):
        rows = full if k < 4 else (h0, h1)[d]
        return same(region(col, z_at(d, k), rows), zs.at[col, d, k - 1], zr.at[col, d, k - 1], (zp, zm)[d])

    def share(col, d, k):
        rows = full if k < 4 else (h0, h1)[d]
        return same(region(col, z_at(d, k), rows), shs.at[col, d, k - 1], shr.at[col, d, k - 1], sib)

    def share_in(col, d, k):
        rows = sfull if k < 4 else (sh0, sh1)[d]
        return same(region(col, z_at(d, k), rows), shs.at[col, d, k - 1], shr.at[col, d, k - 1], sib)

    def share_own(col):
        return same(region(col, z, full), sys_.at[col - 1], syr.at[col - 1], sib)

    def share_own_in(col):
        return same(region(col, z, sfull), sys_.at[col - 1], syr.at[col - 1], sib)

    def z_first(col):
        z_out(col, 0, 1).start()
        z_out(col, 1, 1).start()

    def z_serve(k, cols):
        for col in cols:
            for d in range(2):
                z_in(col, d, k).wait_recv()
                if k < 4:
                    z_out(col, d, k + 1).start()
                share(col, d, k).start()

    wcp.wait()
    for cp in ax_out:
        cp.start()
    z_first(0)

    ACC[...] = jnp.zeros_like(ACC)

    def ssq(g, u):
        tot = jnp.zeros((TOK, 128), F32)
        for i in range(4):
            xcopy(g * 4 + i).wait()
            v = X[g * 4 + i].astype(F32)
            v = v * v
            tot = tot + (v[:, :128] + v[:, 128:])
        ACC[...] += tot
        return u

    lax.fori_loop(0, NCH // 4, ssq, 0)
    mean = jnp.sum(ACC[...], axis=1, keepdims=True) / D
    rstd = lax.rsqrt(mean + 1e-05)
    RB[...] = jnp.broadcast_to(rstd, (TOK, 128))

    for cp in ax_in:
        cp.wait_recv()
    for cp in ay_out[:2]:
        cp.start()
    z_first(1)
    share_own(1).start()

    LT[:, 0:TOK] = live_ref[...].astype(F32).T.astype(BF16)
    lt_copy = rcopy(LT.at[:, 0:TOK], LT.at[:, TOK : 2 * TOK], lts, ltr, sib)
    lt_copy.start()

    def normed(j):
        rb = RB[...]
        v = X[j].astype(F32)
        return (v * jnp.concatenate([rb, rb], axis=1) * gain_ref[j]).astype(BF16)

    def n_copy(i):
        return rcopy(Ns.at[i], Nh.at[i, TOK : 2 * TOK], nss.at[i], nsr.at[i], sib)

    def order(i):
        far = i < 2
        mid = i < 10
        yy = jnp.where(far, (y + 2) % 4, jnp.where(mid, (i - 2) % 4, (y + jnp.where(i < 12, 1, jnp.where(i < 14, 3, 0))) % 4))
        zz = jnp.where(far, 2 + i, jnp.where(mid, (i - 2) // 4, 2 + i % 2))
        return yy, zz

    def norm_sib(i, u):
        yy, zz = order(i)
        Ns[yy * 4 + zz] = normed(yy * 8 + 4 * (1 - c) + zz)
        n_copy(yy * 4 + zz).start()
        return u

    def norm_own(i, u):
        yy, zz = order(i)
        Nh[yy * 4 + zz, 0:TOK] = normed(yy * 8 + 4 * c + zz)
        return u

    lax.fori_loop(0, 16, norm_sib, 0)
    for i in range(2):
        ay_in[i].wait_recv()
        ay_out[2 + i].start()
    for col in (2, 3):
        z_first(col)
        share_own(col).start()
    lax.fori_loop(0, 16, norm_own, 0)
    for cp in ay_in[2:]:
        cp.wait_recv()
    z_first(4)
    share_own(4).start()
    lt_copy.wait_recv()

    def product(i, u):
        yy, zz = order(i)
        at = yy * 4 + zz
        n_copy(at).wait_recv()
        st = jnp.dot(LT[...], Nh[at], preferred_element_type=F32)
        S[at, 0] = st[:, :128]
        S[at, 1] = st[:, 128:]
        return u

    def x_of(rel):
        xx = (x + rel) % 4
        return xx % 2, xx // 2

    def own_1x(rel, h, s):
        l, hi = x_of(rel)
        return S[s * 4 + h, l, pl.ds(pl.multiple_of(256 * hi, 256), 256)]

    def own_1y(rel, h, s):
        return S[((y + rel) % 4) * 4 + 2 + h, s // 2, 256 * (s % 2) : 256 * (s % 2) + 256]

    def own_2y(rel, h, s):
        return A2[h, (y + rel) % 4]

    def own_2x(rel, h, s):
        l, hi = x_of(rel)
        return B2[h, l * 2 + hi]

    r1x = Ring(own_1x, 4, xp, xm, r1x_s, r1x_r, q1xs, q1xr)
    r1y = Ring(own_1y, 4, yp, ym, r1y_s, r1y_r, q1ys, q1yr)
    r2y = Ring(own_2y, 1, yp, ym, r2y_s, r2y_r, q2ys, q2yr)
    r2x = Ring(own_2x, 1, xp, xm, r2x_s, r2x_r, q2xs, q2xr)

    lax.fori_loop(0, 2, product, 0)
    r1y.far(0)
    r1y.far(1)
    lax.fori_loop(2, 6, product, 0)
    r1x.far(0)
    r1x.single(1)
    lax.fori_loop(6, 10, product, 0)
    r1x.far(1)
    r1x.single(0)
    z_serve(1, (0, 1))
    lax.fori_loop(10, 14, product, 0)
    r1y.single(0)
    r1y.single(1)
    lax.fori_loop(14, 16, product, 0)
    z_serve(1, (2, 3))
    r1y.combine(0)
    r1y.combine(1)
    r1x.combine(0)
    r1x.combine(1)
    z_serve(1, (4,))

    ACC[...] = jnp.zeros_like(ACC)

    def ng_chunk(yy, zz):
        j = yy * 8 + zz
        w = Wf[yy, zz].reshape(CH, KW)
        ng = lax.dot_general(live_ref[...], w, (((1,), (1,)), ((), ())), preferred_element_type=F32)
        NG[j] = ng
        v = X[j].astype(F32) * gain_ref[j] * ng
        ACC[...] += v[:, :128] + v[:, 128:]

    for col in (1, 2, 3, 4):
        share_own_in(col).wait_recv()
    lax.fori_loop(0, 4, lambda yy, u: (ng_chunk(yy, z), u)[1], 0)

    def ng_step(k):
        for col in range(5):
            for d in range(2):
                share_in(col, d, k).wait_recv()
        for d in range(2 if k < 4 else 1):
            lax.fori_loop(0, 4, lambda yy, u, d=d: (ng_chunk(yy, z_at(d, k)), u)[1], 0)

    ng_step(1)

    for h in range(2):
        r1y.mine_wait(h)
        for s in range(4):
            B2[h, s] = r1y.mine(h, s)
        r2x.far(h)
        r2x.single(1 - h)
    for h in range(2):
        r1x.mine_wait(h)
        for s in range(4):
            A2[h, s] = r1x.mine(h, s)
        r2y.far(h)
        r2y.single(1 - h)

    z_serve(2, range(5))
    r2x.combine(0)
    r2x.combine(1)
    r2y.combine(0)
    r2y.combine(1)
    ng_step(2)

    for h in range(2):
        r2y.mine_wait(h)
        T[h] = r2y.mine(h, 0)
        r2x.mine_wait(h)
        T[2 + h] = r2x.mine(h, 0)

    def zd_copy(k):
        return rcopy(Tb.at[k], ZR.at[z], zds.at[k], zdr.at[z], dev(x, y, 4 * c + k, c))

    for k in range(4):
        @pl.when(4 * c + k != z)
        def _(k=k):
            Tb[k] = T[k].astype(BF16)
            zd_copy(k).start()

    z_serve(3, range(5))
    ng_step(3)

    owner = z // 4 == c

    def out_copy(i):
        to = (sib, far_same, far_other)[i]
        return rcopy(O.at[xh], O.at[xh], fs.at[i], fr.at[jnp.where(i == 0, 0, 1)], to)

    @pl.when(owner)
    def _():
        tot = T[z % 4]
        for s in range(8):
            @pl.when(s != z)
            def _(s=s):
                rcopy(Tb.at[0], ZR.at[s], zds.at[0], zdr.at[s], sib).wait_recv()
        ZR[z] = jnp.zeros((256, 128), BF16)
        for s in range(8):
            tot = tot + ZR[s].astype(F32)
        O[xh] = (tot / jnp.sqrt(F32(TOKENS))).T
        for i in range(3):
            out_copy(i).start()

    z_serve(4, range(5))
    ng_step(4)

    inner = jnp.sum(ACC[...], axis=1, keepdims=True)
    rb = RB[...]
    ACC[...] = rb * rb * rb * jnp.broadcast_to(inner, (TOK, 128)) / D

    def o_copy(j):
        return pltpu.make_async_copy(X.at[j], ig_hbm.at[:, pl.ds(pl.multiple_of(j * CH, CH), CH)], osem.at[j])

    def last(j, u):
        rb, co = RB[...], ACC[...]
        v = X[j].astype(F32)
        g = gain_ref[j]
        out = jnp.concatenate([rb, rb], axis=1) * g * NG[j] - v * jnp.concatenate([co, co], axis=1)
        X[j] = out.astype(BF16)
        o_copy(j).start()
        return u

    lax.fori_loop(0, NCH, last, 0)

    @pl.when(jnp.logical_not(owner))
    def _():
        rcopy(O.at[xh], O.at[xh], fs.at[0], fr.at[0], sib).wait_recv()

    rcopy(O.at[1 - xh], O.at[1 - xh], fs.at[1], fr.at[1], far_same).wait_recv()
    wg_ref[:, 0:256] = O[0]
    wg_ref[:, 256:512] = O[1]

    @pl.when(owner)
    def _():
        for i in range(3):
            out_copy(i).wait_send()

    for k in range(4):
        @pl.when(4 * c + k != z)
        def _(k=k):
            zd_copy(k).wait_send()
    for ring in (r1x, r1y, r2x, r2y):
        ring.finish()
    for cp in ax_out + ay_out:
        cp.wait_send()
    for col in range(5):
        for d in range(2):
            for k in range(1, 5):
                z_out(col, d, k).wait_send()
                share(col, d, k).wait_send()
    for col in range(1, 5):
        share_own(col).wait_send()
    lt_copy.wait_send()
    lax.fori_loop(0, 16, lambda i, u: (n_copy(i).wait_send(), u)[1], 0)
    lax.fori_loop(0, NCH, lambda j, u: (o_copy(j).wait(), u)[1], 0)


def on_device(layer_input, norm_gain, key_cotangent, segment_ids, key_weight):
    live = jnp.where((segment_ids != 0)[:, None], key_cotangent, jnp.zeros_like(key_cotangent))
    gain = norm_gain.astype(F32).reshape(NCH, 1, CH)
    dma = pltpu.SemaphoreType.DMA
    vm = pltpu.VMEM

    def ring(subs, dtype):
        return [vm((6, subs, 256, 128), dtype)] * 2

    scratch = [
        vm((NCH, TOK, CH), BF16),
        vm((NY, NZ, 2, 128, KW), BF16),
        vm((16, 2 * TOK, CH), BF16),
        vm((16, TOK, CH), BF16),
        vm((KW, 2 * TOK), BF16),
        vm((16, 2, KW, 128), F32),
        vm((NCH, TOK, CH), F32),
        vm((TOK, 128), F32),
        vm((TOK, 128), F32),
        vm((2, 4, 256, 128), F32),
        vm((2, 4, 256, 128), F32),
        vm((4, 256, 128), F32),
        vm((4, 256, 128), BF16),
        vm((8, 256, 128), BF16),
        vm((2, 128, 256), F32),
        *ring(4, BF16), *ring(4, BF16), *ring(1, F32), *ring(1, F32),
        dma((NCH,)), dma, dma((NCH,)), dma((16,)), dma((16,)), dma, dma,
        dma((2,)), dma((2,)), dma((4,)), dma((4,)),
        dma((5, 2, 4)), dma((5, 2, 4)), dma((5, 2, 4)), dma((5, 2, 4)), dma((4,)), dma((4,)),
        *[dma((6,))] * 8,
        dma((4,)), dma((8,)), dma((3,)), dma((2,)),
    ]
    anyspace = pl.BlockSpec(memory_space=pl.ANY)
    vspace = pl.BlockSpec(memory_space=pltpu.VMEM)
    return pl.pallas_call(
        kernel,
        name="key_projection_backward",
        out_shape=(jax.ShapeDtypeStruct((128, KW), F32), jax.ShapeDtypeStruct((TOK, D), BF16)),
        in_specs=[anyspace, vspace, vspace, anyspace],
        out_specs=(vspace, anyspace),
        scratch_shapes=scratch,
        compiler_params=pltpu.CompilerParams(
            collective_id=0, has_side_effects=True, vmem_limit_bytes=62 * 2**20
        ),
    )(layer_input, gain, live, key_weight)


def solution(mesh):
    placed = (
        P(("blk", "rep"), None),
        P(),
        P(("blk", "rep"), None),
        P(("blk", "rep")),
        P("blk", None),
    )
    return jax.shard_map(
        on_device,
        mesh=mesh,
        in_specs=placed,
        out_specs=(P("blk", None), P(("blk", "rep"), None)),
        check_vma=False,
    )
```

```python
import jax
import jax.numpy as jnp
from jax import lax
from jax.experimental import pallas as pl
from jax.experimental.pallas import tpu as pltpu
from jax.sharding import PartitionSpec as P

F32 = jnp.float32
BF16 = jnp.bfloat16
NX, NY, NZ = 4, 4, 8
TOK, D, KW, TOKENS = 384, 8192, 512, 98304
CH = 256
NCH = D // CH


def dev(x, y, z, c):
    return {"blk": (y * NZ + z) * 2 + x % 2, "rep": (x // 2) * 2 + c}


class Ring:
    def __init__(self, own, subs, plus, minus, send, recv, ssem, rsem):
        self.own, self.subs, self.to = own, subs, (plus, minus)
        self.send, self.recv, self.ssem, self.rsem = send, recv, ssem, rsem

    def copy(self, i):
        return pltpu.make_async_remote_copy(
            self.send.at[i], self.recv.at[i], self.ssem.at[i], self.rsem.at[i], device_id=self.to[i % 2]
        )

    def put(self, i, rel, h, plus=None):
        for s in range(self.subs):
            v = self.own(rel, h, s)
            if plus is not None:
                v = v + self.recv[plus, s].astype(F32)
            self.send[i, s] = v.astype(self.send.dtype)
        self.copy(i).start()

    def far(self, h):
        self.put(h, 2, h)

    def single(self, d):
        self.put(2 + d, (1, 3)[d], (1, 0)[d])

    def combine(self, d):
        self.copy(d).wait_recv()
        self.put(4 + d, (1, 3)[d], d, plus=d)

    def mine_wait(self, h):
        for i in ((4, 3), (2, 5))[h]:
            self.copy(i).wait_recv()

    def mine(self, h, s):
        a, b = ((4, 3), (2, 5))[h]
        return self.own(0, h, s) + self.recv[a, s].astype(F32) + self.recv[b, s].astype(F32)

    def finish(self):
        for i in range(6):
            self.copy(i).wait_send()


def kernel(
    x_hbm, gain_ref, kc_hbm, seg_ref, w_hbm, wg_ref, X,
    kc_ref, G, live_ref, Wf, Nh, Ns, LT, S, NG, ACC, RB, A2, B2, T, Tb, ZR, O,
    r1x_s, r1x_r, r1y_s, r1y_r, r2y_s, r2y_r, r2x_s, r2x_r,
    xsem, wsem, kcsem, nss, nsr, lts, ltr,
    axs, axr, ays, ayr, zs, zr, shs, shr, sys_, syr,
    q1xs, q1xr, q1ys, q1yr, q2ys, q2yr, q2xs, q2xr,
    zds, zdr, fs, fr,
):
    b, r = lax.axis_index("blk"), lax.axis_index("rep")
    xl, z, y = b % 2, (b // 2) % NZ, b // (2 * NZ)
    xh, c = r // 2, r % 2
    x = 2 * xh + xl
    sib = dev(x, y, z, 1 - c)
    xp, xm = dev((x + 1) % 4, y, z, c), dev((x + 3) % 4, y, z, c)
    yp, ym = dev(x, (y + 1) % 4, z, c), dev(x, (y + 3) % 4, z, c)
    zp, zm = dev(x, y, (z + 1) % 8, c), dev(x, y, (z + 7) % 8, c)
    far_same, far_other = dev((x + 2) % 4, y, z, c), dev((x + 2) % 4, y, z, 1 - c)

    wcp = pltpu.make_async_copy(w_hbm.at[:, pl.ds(pl.multiple_of(256 * c, 256), 256)], Wf.at[c, y, z, xl], wsem)
    wcp.start()
    kcp = pltpu.make_async_copy(kc_hbm, kc_ref, kcsem)
    kcp.start()

    def xcopy(j):
        return pltpu.make_async_copy(x_hbm.at[:, pl.ds(pl.multiple_of(j * CH, CH), CH)], X.at[j], xsem.at[j])

    bar = pltpu.get_barrier_semaphore()
    met = [sib, xp, xm, yp, ym, dev(x, (y + 2) % 4, z, c), far_same, far_other] + [dev(x, y, (z + k) % 8, c) for k in range(1, 8)]
    for d in met:
        pl.semaphore_signal(bar, 1, device_id=d)

    lax.fori_loop(0, NCH, lambda j, u: (xcopy(j).start(), u)[1], 0)
    pl.semaphore_wait(bar, len(met))
    full, h0, h1 = pl.ds(0, 128), pl.ds(0, 64), pl.ds(64, 64)
    cols = ((0, 0), (0, 1), (1, 0), (3, 0), (2, 0), (1, 1), (3, 1), (2, 1))

    def region(col, zz, rows, half=c):
        back, other = cols[col]
        return Wf.at[half, (y + 4 - back) % 4, zz, 1 - xl if other else xl, rows]

    def rcopy(src, dst, ss, rs, to):
        return pltpu.make_async_remote_copy(src, dst, ss, rs, device_id=to)

    def same(ref, ss, rs, to):
        return rcopy(ref, ref, ss, rs, to)

    ax_out = [same(region(0, z, h0), axs.at[0], axr.at[0], xp), same(region(0, z, h1), axs.at[1], axr.at[1], xm)]
    ax_in = [same(region(1, z, h0), axs.at[0], axr.at[0], xp), same(region(1, z, h1), axs.at[1], axr.at[1], xm)]
    def ay(col):
        back, other = cols[col]
        src = region(other, z, full)
        return same(src, ays.at[col - 2], ayr.at[col - 2], dev(x, (y + back) % 4, z, c))

    def ay_in(col):
        return same(region(col, z, full), ays.at[col - 2], ayr.at[col - 2], yp)

    def ay_serve(col):
        ay_in(col).wait_recv()
        z_first(col)
        share_own(col).start()

    def z_at(d, k):
        return (z + 8 - k) % 8 if d == 0 else (z + k) % 8

    def z_out(col, d, k):
        rows = full if k < 4 else (h0, h1)[d]
        return same(region(col, z_at(d, k - 1), rows), zs.at[col, d, k - 1], zr.at[col, d, k - 1], (zp, zm)[d])

    def z_in(col, d, k):
        rows = full if k < 4 else (h0, h1)[d]
        return same(region(col, z_at(d, k), rows), zs.at[col, d, k - 1], zr.at[col, d, k - 1], (zp, zm)[d])

    def share(col, d, k):
        rows = full if k < 4 else (h0, h1)[d]
        return same(region(col, z_at(d, k), rows), shs.at[col, d, k - 1], shr.at[col, d, k - 1], sib)

    def share_in(col, d, k):
        rows = full if k < 4 else (h0, h1)[d]
        return same(region(col, z_at(d, k), rows, 1 - c), shs.at[col, d, k - 1], shr.at[col, d, k - 1], sib)

    def share_own(col):
        return same(region(col, z, full), sys_.at[col], syr.at[col], sib)

    def share_own_in(col):
        return same(region(col, z, full, 1 - c), sys_.at[col], syr.at[col], sib)

    def z_first(col):
        z_out(col, 0, 1).start()
        z_out(col, 1, 1).start()

    def z_serve(k, cols):
        for col in cols:
            for d in range(2):
                z_in(col, d, k).wait_recv()
                if k < 4:
                    z_out(col, d, k + 1).start()
                share(col, d, k).start()

    wcp.wait()
    for cp in ax_out:
        cp.start()
    z_first(0)
    for col in (2, 3, 4):
        ay(col).start()
    share_own(0).start()

    kcp.wait()
    row = jnp.where(seg_ref[...].reshape(1, TOK) != 0, F32(1), F32(0))
    tall = jnp.broadcast_to(row, (128, TOK)).T
    kcv = kc_ref[...].astype(F32)
    live = jnp.where(jnp.concatenate([tall] * 4, axis=1) != 0, kcv, F32(0))
    live_ref[...] = live.astype(BF16)
    LT[:, 0:TOK] = live.T.astype(BF16)
    for j in range(NCH):
        G[j] = gain_ref[CH * j : CH * (j + 1)].astype(F32).reshape(1, CH)
    lt_copy = pltpu.make_async_remote_copy(
        LT.at[:, 0:TOK], LT.at[:, TOK : 2 * TOK], lts, ltr, device_id=sib
    )
    lt_copy.start()

    for cp in ax_in:
        cp.wait_recv()
    z_first(1)
    for col in (5, 6, 7):
        ay(col).start()
    share_own(1).start()

    ACC[...] = jnp.zeros_like(ACC)

    def ssq(g, u):
        tot = jnp.zeros((TOK, 128), F32)
        for i in range(4):
            xcopy(g * 4 + i).wait()
            v = X[g * 4 + i].astype(F32)
            v = v * v
            tot = tot + (v[:, :128] + v[:, 128:])
        ACC[...] += tot
        return u

    lax.fori_loop(0, NCH // 4, ssq, 0)
    mean = jnp.sum(ACC[...], axis=1, keepdims=True) / D
    rstd = lax.rsqrt(mean + 1e-05)
    RB[...] = jnp.broadcast_to(rstd, (TOK, 128))

    for col in (2, 3, 4):
        ay_serve(col)

    def normed(j):
        rb = RB[...]
        v = X[j].astype(F32)
        return (v * jnp.concatenate([rb, rb], axis=1) * G[j]).astype(BF16)

    def n_copy(i):
        return rcopy(Ns.at[i], Nh.at[i, TOK : 2 * TOK], nss.at[i], nsr.at[i], sib)

    def order(i):
        far = i < 2
        mid = i < 10
        yy = jnp.where(far, (y + 2) % 4, jnp.where(mid, (i - 2) % 4, (y + jnp.where(i < 12, 1, jnp.where(i < 14, 3, 0))) % 4))
        zz = jnp.where(far, 2 + i, jnp.where(mid, (i - 2) // 4, 2 + i % 2))
        return yy, zz

    def norm_sib(i, u):
        yy, zz = order(i)
        Ns[yy * 4 + zz] = normed(yy * 8 + 4 * (1 - c) + zz)
        n_copy(yy * 4 + zz).start()
        return u

    def norm_own(i, u):
        yy, zz = order(i)
        Nh[yy * 4 + zz, 0:TOK] = normed(yy * 8 + 4 * c + zz)
        return u

    lax.fori_loop(0, 16, norm_sib, 0)
    for col in (5, 6, 7):
        ay_serve(col)
    lax.fori_loop(0, 16, norm_own, 0)
    lt_copy.wait_recv()

    def product(i, u):
        yy, zz = order(i)
        at = yy * 4 + zz
        n_copy(at).wait_recv()
        st = jnp.dot(LT[...], Nh[at], preferred_element_type=F32)
        S[at, 0] = st[:, :128]
        S[at, 1] = st[:, 128:]
        return u

    def x_of(rel):
        xx = (x + rel) % 4
        return xx % 2, xx // 2

    def part(first, b):
        return pl.ds(pl.multiple_of(first + 128 * b, 128), 128)

    def rings(b):
        def own_1x(rel, h, s):
            l, hi = x_of(rel)
            return S[s * 4 + h, l, part(256 * hi, b)]

        def own_1y(rel, h, s):
            return S[((y + rel) % 4) * 4 + 2 + h, s // 2, part(256 * (s % 2), b)]

        def own_2y(rel, h, s):
            return A2[h, (y + rel) % 4, part(0, b)]

        def own_2x(rel, h, s):
            l, hi = x_of(rel)
            return B2[h, l * 2 + hi, part(0, b)]

        return (
            Ring(own_1x, 4, xp, xm, r1x_s.at[b], r1x_r.at[b], q1xs.at[b], q1xr.at[b]),
            Ring(own_1y, 4, yp, ym, r1y_s.at[b], r1y_r.at[b], q1ys.at[b], q1yr.at[b]),
            Ring(own_2x, 1, xp, xm, r2x_s.at[b], r2x_r.at[b], q2xs.at[b], q2xr.at[b]),
            Ring(own_2y, 1, yp, ym, r2y_s.at[b], r2y_r.at[b], q2ys.at[b], q2yr.at[b]),
        )

    every = [rings(0), rings(1)]

    def far(ring):
        ring.far(0)
        ring.far(1)

    def single(ring):
        ring.single(0)
        ring.single(1)

    def combine(ring):
        ring.combine(0)
        ring.combine(1)

    def zd_copy(k, b):
        return rcopy(Tb.at[k, part(0, b)], ZR.at[z, part(0, b)], zds.at[b, k], zdr.at[b, z], dev(x, y, 4 * c + k, c))

    def third(b):
        _, _, r2x, r2y = every[b]
        for h in range(2):
            r2y.mine_wait(h)
            T[h, part(0, b)] = r2y.mine(h, 0)
            r2x.mine_wait(h)
            T[2 + h, part(0, b)] = r2x.mine(h, 0)
        for k in range(4):
            @pl.when(4 * c + k != z)
            def _(k=k):
                Tb[k, part(0, b)] = T[k, part(0, b)].astype(BF16)
                zd_copy(k, b).start()

    owner = z // 4 == c

    def out_copy(i, b):
        to = (sib, far_same, far_other)[i]
        return rcopy(O.at[xh, b], O.at[xh, b], fs.at[b, i], fr.at[b, jnp.where(i == 0, 0, 1)], to)

    def fourth(b):
        @pl.when(owner)
        def _():
            for s in range(8):
                @pl.when(s != z)
                def _(s=s):
                    rcopy(Tb.at[0, part(0, b)], ZR.at[s, part(0, b)], zds.at[b, 0], zdr.at[b, s], sib).wait_recv()
            ZR[z, part(0, b)] = jnp.zeros((128, 128), BF16)
            tot = T[z % 4, part(0, b)]
            for s in range(8):
                tot = tot + ZR[s, part(0, b)].astype(F32)
            O[xh, b] = (tot / jnp.sqrt(F32(TOKENS))).T
            for i in range(3):
                out_copy(i, b).start()

    r1x, r1y, r2x, r2y = every[0]
    q1x, q1y, q2x, q2y = every[1]
    lax.fori_loop(0, 2, product, 0)
    far(r1y)
    lax.fori_loop(2, 6, product, 0, unroll=2)
    r1x.far(0)
    z_serve(1, (0, 1, 2))
    lax.fori_loop(6, 10, product, 0, unroll=2)
    r1x.far(1)
    single(r1x)
    lax.fori_loop(10, 16, product, 0, unroll=2)
    single(r1y)
    z_serve(1, (3, 4, 5))
    combine(r1y)
    far(q1y)
    single(q1y)
    combine(r1x)
    far(q1x)
    single(q1x)
    z_serve(1, (6, 7))

    ACC[...] = jnp.zeros_like(ACC)

    def ng_chunk(yy, zz):
        j = yy * 8 + zz
        nt = (((1,), (1,)), ((), ()))
        ng = lax.dot_general(live_ref[:, 0:256], Wf[0, yy, zz].reshape(CH, 256), nt, preferred_element_type=F32)
        ng += lax.dot_general(live_ref[:, 256:512], Wf[1, yy, zz].reshape(CH, 256), nt, preferred_element_type=F32)
        NG[j] = ng
        v = X[j].astype(F32) * G[j] * ng
        ACC[...] += v[:, :128] + v[:, 128:]

    def ng_chunks(zz):
        lax.fori_loop(0, 4, lambda yy, u: (ng_chunk(yy, zz), u)[1], 0, unroll=True)

    def ng_step(k):
        for col in range(8):
            for d in range(2):
                share_in(col, d, k).wait_recv()
        for d in range(2 if k < 4 else 1):
            ng_chunks(z_at(d, k))

    def second(rings_b, b, along_y):
        r1x, r1y, r2x, r2y = rings_b
        one, two, to = (r1y, r2x, B2) if along_y else (r1x, r2y, A2)
        for h in range(2):
            one.mine_wait(h)
            for s in range(4):
                to[h, s, part(0, b)] = one.mine(h, s)
        far(two)
        single(two)

    combine(q1y)
    second(every[0], 0, True)
    z_serve(2, (0, 1, 2))
    combine(q1x)
    second(every[0], 0, False)
    z_serve(2, (3, 4, 5))
    for col in range(8):
        share_own_in(col).wait_recv()
    ng_chunks(z)
    combine(r2x)
    combine(r2y)
    z_serve(2, (6, 7))
    ng_step(1)
    second(every[1], 1, True)
    second(every[1], 1, False)
    z_serve(3, (0, 1, 2))
    ng_step(2)
    third(0)
    z_serve(3, (3, 4, 5))
    combine(q2x)
    combine(q2y)
    z_serve(3, (6, 7))
    ng_step(3)
    third(1)
    fourth(0)
    z_serve(4, range(8))
    ng_step(4)
    fourth(1)

    inner = jnp.sum(ACC[...], axis=1, keepdims=True)
    rb = RB[...]
    ACC[...] = rb * rb * rb * jnp.broadcast_to(inner, (TOK, 128)) / D

    def last(j, u):
        rb, co = RB[...], ACC[...]
        v = X[j].astype(F32)
        g = G[j]
        out = jnp.concatenate([rb, rb], axis=1) * g * NG[j] - v * jnp.concatenate([co, co], axis=1)
        X[j] = out.astype(BF16)
        return u

    lax.fori_loop(0, NCH, last, 0)

    for b in range(2):
        @pl.when(jnp.logical_not(owner))
        def _(b=b):
            rcopy(O.at[xh, b], O.at[xh, b], fs.at[b, 0], fr.at[b, 0], sib).wait_recv()

        rcopy(O.at[1 - xh, b], O.at[1 - xh, b], fs.at[b, 1], fr.at[b, 1], far_same).wait_recv()
        wg_ref[:, 128 * b : 128 * b + 128] = O[0, b]
        wg_ref[:, 256 + 128 * b : 384 + 128 * b] = O[1, b]

        @pl.when(owner)
        def _(b=b):
            for i in range(3):
                out_copy(i, b).wait_send()

        for k in range(4):
            @pl.when(4 * c + k != z)
            def _(k=k, b=b):
                zd_copy(k, b).wait_send()
        for ring in every[b]:
            ring.finish()
    for cp in ax_out:
        cp.wait_send()
    for col in range(2, 8):
        ay(col).wait_send()
    for col in range(8):
        for d in range(2):
            for k in range(1, 5):
                z_out(col, d, k).wait_send()
                share(col, d, k).wait_send()
    for col in range(8):
        share_own(col).wait_send()
    lt_copy.wait_send()
    lax.fori_loop(0, 16, lambda i, u: (n_copy(i).wait_send(), u)[1], 0)


def copy_out(ig, wg, ig_out, wg_out, sem):
    cps = [pltpu.make_async_copy(ig.at[j], ig_out.at[:, pl.ds(j * CH, CH)], sem.at[j]) for j in range(NCH)]
    cps.append(pltpu.make_async_copy(wg, wg_out, sem.at[NCH]))
    for cp in cps:
        cp.start()
    for cp in cps:
        cp.wait()


def on_device(layer_input, norm_gain, key_cotangent, segment_ids, key_weight):
    dma = pltpu.SemaphoreType.DMA
    vm = pltpu.VMEM

    def ring(subs, dtype):
        return [vm((2, 6, subs, 128, 128), dtype)] * 2

    scratch = [
        vm((TOK, KW), BF16),
        vm((NCH, 1, CH), F32),
        vm((TOK, KW), BF16),
        vm((2, NY, NZ, 2, 128, 256), BF16),
        vm((16, 2 * TOK, CH), BF16),
        vm((16, TOK, CH), BF16),
        vm((KW, 2 * TOK), BF16),
        vm((16, 2, KW, 128), F32),
        vm((NCH, TOK, CH), F32),
        vm((TOK, 128), F32),
        vm((TOK, 128), F32),
        vm((2, 4, 256, 128), F32),
        vm((2, 4, 256, 128), F32),
        vm((4, 256, 128), F32),
        vm((4, 256, 128), BF16),
        vm((8, 256, 128), BF16),
        vm((2, 2, 128, 128), F32),
        *ring(4, BF16), *ring(4, BF16), *ring(1, F32), *ring(1, F32),
        dma((NCH,)), dma, dma, dma((16,)), dma((16,)), dma, dma,
        dma((2,)), dma((2,)), dma((6,)), dma((6,)),
        dma((8, 2, 4)), dma((8, 2, 4)), dma((8, 2, 4)), dma((8, 2, 4)), dma((8,)), dma((8,)),
        *[dma((2, 6))] * 8,
        dma((2, 4)), dma((2, 8)), dma((2, 3)), dma((2, 2)),
    ]
    anyspace = pl.BlockSpec(memory_space=pl.ANY)
    vspace = pl.BlockSpec(memory_space=pltpu.VMEM)
    wg, ig = pl.pallas_call(
        kernel,
        name="key_projection_backward",
        out_shape=(pltpu.VMEM((128, KW), F32), pltpu.VMEM((NCH, TOK, CH), BF16)),
        in_specs=[anyspace, vspace, anyspace, vspace, anyspace],
        out_specs=(vspace, vspace),
        scratch_shapes=scratch,
        compiler_params=pltpu.CompilerParams(
            collective_id=0, has_side_effects=True, vmem_limit_bytes=53 * 2**20
        ),
    )(layer_input, norm_gain, key_cotangent, segment_ids, key_weight)
    ig, wg = pl.pallas_call(
        copy_out,
        name="copy_out",
        out_shape=(jax.ShapeDtypeStruct((TOK, D), BF16), jax.ShapeDtypeStruct((128, KW), F32)),
        in_specs=[vspace] * 2,
        out_specs=(anyspace,) * 2,
        scratch_shapes=[dma((NCH + 1,))],
        compiler_params=pltpu.CompilerParams(vmem_limit_bytes=2**20),
    )(pltpu.with_memory_space_constraint(ig, pltpu.VMEM), pltpu.with_memory_space_constraint(wg, pltpu.VMEM))
    return wg, ig


def solution(mesh):
    placed = (
        P(("blk", "rep"), None),
        P(),
        P(("blk", "rep"), None),
        P(("blk", "rep")),
        P("blk", None),
    )
    return jax.shard_map(
        on_device,
        mesh=mesh,
        in_specs=placed,
        out_specs=(P("blk", None), P(("blk", "rep"), None)),
        check_vma=False,
    )
```

```python
import jax
import jax.numpy as jnp
from jax import lax
from jax.experimental import pallas as pl
from jax.experimental.pallas import tpu as pltpu
from jax.sharding import PartitionSpec as P

F32 = jnp.float32
BF16 = jnp.bfloat16
NX, NY, NZ = 4, 4, 8
TOK, D, KW, TOKENS = 384, 8192, 512, 98304
CH = 256
NCH = D // CH
AHEAD = 6


def dev(x, y, z, c):
    return {"blk": (y * NZ + z) * 2 + x % 2, "rep": (x // 2) * 2 + c}


class Ring:
    def __init__(self, own, subs, plus, minus, send, recv, ssem, rsem):
        self.own, self.subs, self.to = own, subs, (plus, minus)
        self.send, self.recv, self.ssem, self.rsem = send, recv, ssem, rsem

    def copy(self, i):
        src, dst = (bufs[i // 4].at[i % 4] for bufs in (self.send, self.recv))
        return pltpu.make_async_remote_copy(src, dst, self.ssem.at[i], self.rsem.at[i], device_id=self.to[i % 2])

    def got(self, i, s):
        return self.recv[i // 4][i % 4, s].astype(F32)

    def put(self, i, rel, h, plus=None):
        for s in range(self.subs):
            v = self.own(rel, h, s)
            if plus is not None:
                v = v + self.got(plus, s)
            ref = self.send[i // 4]
            ref[i % 4, s] = v.astype(ref.dtype)
        self.copy(i).start()

    def far(self, h):
        self.put(h, 2, h)

    def single(self, d):
        self.put(2 + d, (1, 3)[d], (1, 0)[d])

    def combine(self, d):
        self.copy(d).wait_recv()
        self.put(4 + d, (1, 3)[d], d, plus=d)

    def mine_wait(self, h):
        for i in ((4, 3), (2, 5))[h]:
            self.copy(i).wait_recv()

    def mine(self, h, s):
        a, b = ((4, 3), (2, 5))[h]
        return self.own(0, h, s) + self.got(a, s) + self.got(b, s)

    def finish(self):
        for i in range(6):
            self.copy(i).wait_send()


def kernel(
    x_hbm, gain_ref, kc_hbm, seg_ref, w_hbm, wg_ref, X,
    kc_ref, G, live_ref, Wf, Nh, Ns, LT, S, NG, ACC, RB, A2, B2, T, Tb, ZR, O,
    r1x_s, r1x_r, r1y_s, r1y_r, r2y_s, r2y_r, r2x_s, r2x_r,
    c1x_s, c1x_r, c1y_s, c1y_r, c2y_s, c2y_r, c2x_s, c2x_r,
    xsem, wsem, kcsem, nss, nsr, lts, ltr,
    axs, axr, ays, ayr, zs, zr, shs, shr, sys_, syr,
    q1xs, q1xr, q1ys, q1yr, q2ys, q2yr, q2xs, q2xr,
    zds, zdr, fs, fr,
):
    b, r = lax.axis_index("blk"), lax.axis_index("rep")
    xl, z, y = b % 2, (b // 2) % NZ, b // (2 * NZ)
    xh, c = r // 2, r % 2
    x = 2 * xh + xl
    sib = dev(x, y, z, 1 - c)
    xp, xm = dev((x + 1) % 4, y, z, c), dev((x + 3) % 4, y, z, c)
    yp, ym = dev(x, (y + 1) % 4, z, c), dev(x, (y + 3) % 4, z, c)
    zp, zm = dev(x, y, (z + 1) % 8, c), dev(x, y, (z + 7) % 8, c)
    far_same, far_other = dev((x + 2) % 4, y, z, c), dev((x + 2) % 4, y, z, 1 - c)

    wcp = pltpu.make_async_copy(w_hbm.at[:, pl.ds(pl.multiple_of(256 * c, 256), 256)], Wf.at[c, y, z, xl], wsem)
    wcp.start()
    kcp = pltpu.make_async_copy(kc_hbm, kc_ref, kcsem)
    kcp.start()

    def xcopy(j):
        return pltpu.make_async_copy(x_hbm.at[:, pl.ds(pl.multiple_of(j * CH, CH), CH)], X.at[j], xsem.at[j])

    bar = pltpu.get_barrier_semaphore()
    met = [sib, xp, xm, yp, ym, dev(x, (y + 2) % 4, z, c), far_same, far_other] + [dev(x, y, (z + k) % 8, c) for k in range(1, 8)]
    for d in met:
        pl.semaphore_signal(bar, 1, device_id=d)

    lax.fori_loop(0, NCH, lambda j, u: (xcopy(j).start(), u)[1], 0)
    pl.semaphore_wait(bar, len(met))
    full, h0, h1 = pl.ds(0, 128), pl.ds(0, 64), pl.ds(64, 64)
    cols = ((0, 0), (0, 1), (1, 0), (3, 0), (2, 0), (1, 1), (3, 1), (2, 1))

    def region(col, zz, rows, half=c):
        back, other = cols[col]
        return Wf.at[half, (y + 4 - back) % 4, zz, 1 - xl if other else xl, rows]

    def rcopy(src, dst, ss, rs, to):
        return pltpu.make_async_remote_copy(src, dst, ss, rs, device_id=to)

    def same(ref, ss, rs, to):
        return rcopy(ref, ref, ss, rs, to)

    ax_out = [same(region(0, z, h0), axs.at[0], axr.at[0], xp), same(region(0, z, h1), axs.at[1], axr.at[1], xm)]
    ax_in = [same(region(1, z, h0), axs.at[0], axr.at[0], xp), same(region(1, z, h1), axs.at[1], axr.at[1], xm)]
    def ay(col):
        back, other = cols[col]
        src = region(other, z, full)
        return same(src, ays.at[col - 2], ayr.at[col - 2], dev(x, (y + back) % 4, z, c))

    def ay_in(col):
        return same(region(col, z, full), ays.at[col - 2], ayr.at[col - 2], yp)

    def ay_serve(col):
        ay_in(col).wait_recv()
        z_first(col)
        share_own(col).start()

    def z_at(d, k):
        return (z + 8 - k) % 8 if d == 0 else (z + k) % 8

    def z_out(col, d, k):
        rows = full if k < 4 else (h0, h1)[d]
        return same(region(col, z_at(d, k - 1), rows), zs.at[col, d, k - 1], zr.at[col, d, k - 1], (zp, zm)[d])

    def z_in(col, d, k):
        rows = full if k < 4 else (h0, h1)[d]
        return same(region(col, z_at(d, k), rows), zs.at[col, d, k - 1], zr.at[col, d, k - 1], (zp, zm)[d])

    def share(col, d, k):
        rows = full if k < 4 else (h0, h1)[d]
        return same(region(col, z_at(d, k), rows), shs.at[col, d, k - 1], shr.at[col, d, k - 1], sib)

    def share_in(col, d, k):
        rows = full if k < 4 else (h0, h1)[d]
        return same(region(col, z_at(d, k), rows, 1 - c), shs.at[col, d, k - 1], shr.at[col, d, k - 1], sib)

    def share_own(col):
        return same(region(col, z, full), sys_.at[col], syr.at[col], sib)

    def share_own_in(col):
        return same(region(col, z, full, 1 - c), sys_.at[col], syr.at[col], sib)

    def z_first(col):
        z_out(col, 0, 1).start()
        z_out(col, 1, 1).start()

    def z_serve(k, cols):
        for col in cols:
            for d in range(2):
                z_in(col, d, k).wait_recv()
                if k < 4:
                    z_out(col, d, k + 1).start()
                share(col, d, k).start()

    wcp.wait()
    for cp in ax_out:
        cp.start()
    z_first(0)
    for col in (2, 3, 4):
        ay(col).start()
    share_own(0).start()

    kcp.wait()
    row = jnp.where(seg_ref[...].reshape(1, TOK) != 0, F32(1), F32(0))
    tall = jnp.broadcast_to(row, (128, TOK)).T
    kcv = kc_ref[...].astype(F32)
    live = jnp.where(jnp.concatenate([tall] * 4, axis=1) != 0, kcv, F32(0))
    live_ref[...] = live.astype(BF16)
    LT[:, 0:TOK] = live.T.astype(BF16)
    for j in range(NCH):
        G[j] = gain_ref[CH * j : CH * (j + 1)].astype(F32).reshape(1, CH)
    lt_copy = pltpu.make_async_remote_copy(
        LT.at[:, 0:TOK], LT.at[:, TOK : 2 * TOK], lts, ltr, device_id=sib
    )
    lt_copy.start()

    for cp in ax_in:
        cp.wait_recv()
    z_first(1)
    for col in (5, 6, 7):
        ay(col).start()
    share_own(1).start()

    ACC[...] = jnp.zeros_like(ACC)

    def ssq(g, u):
        tot = jnp.zeros((TOK, 128), F32)
        for i in range(4):
            xcopy(g * 4 + i).wait()
            v = X[g * 4 + i].astype(F32)
            v = v * v
            tot = tot + (v[:, :128] + v[:, 128:])
        ACC[...] += tot
        return u

    lax.fori_loop(0, NCH // 4, ssq, 0)
    mean = jnp.sum(ACC[...], axis=1, keepdims=True) / D
    rstd = lax.rsqrt(mean + 1e-05)
    RB[...] = jnp.broadcast_to(rstd, (TOK, 128))

    for col in (2, 3, 4):
        ay_serve(col)

    def normed(j):
        rb = RB[...]
        v = X[j].astype(F32)
        return (v * jnp.concatenate([rb, rb], axis=1) * G[j]).astype(BF16)

    def n_copy(i):
        return rcopy(Ns.at[i], Nh.at[i, TOK : 2 * TOK], nss.at[i], nsr.at[i], sib)

    def order(i):
        far = i < 2
        mid = i < 10
        yy = jnp.where(far, (y + 2) % 4, jnp.where(mid, (i - 2) % 4, (y + jnp.where(i < 12, 1, jnp.where(i < 14, 3, 0))) % 4))
        zz = jnp.where(far, 2 + i, jnp.where(mid, (i - 2) // 4, 2 + i % 2))
        return yy, zz

    def norm_sib(i, u):
        yy, zz = order(i)
        Ns[yy * 4 + zz] = normed(yy * 8 + 4 * (1 - c) + zz)
        n_copy(yy * 4 + zz).start()
        return u

    def norm_own(i, u):
        yy, zz = order(i)
        Nh[yy * 4 + zz, 0:TOK] = normed(yy * 8 + 4 * c + zz)
        return u

    def norm_both(i, u):
        norm_sib(i, u)
        return norm_own(i, u)

    lax.fori_loop(0, AHEAD, norm_both, 0)
    for col in (5, 6, 7):
        ay_serve(col)
    lt_copy.wait_recv()

    def product(i, u):
        yy, zz = order(i)
        at = yy * 4 + zz
        n_copy(at).wait_recv()
        st = jnp.dot(LT[...], Nh[at], preferred_element_type=F32)
        S[at, 0] = st[:, :128]
        S[at, 1] = st[:, 128:]
        return u

    def x_of(rel):
        xx = (x + rel) % 4
        return xx % 2, xx // 2

    def part(first, b):
        return pl.ds(pl.multiple_of(first + 128 * b, 128), 128)

    def rings(b):
        def own_1x(rel, h, s):
            l, hi = x_of(rel)
            return S[s * 4 + h, l, part(256 * hi, b)]

        def own_1y(rel, h, s):
            return S[((y + rel) % 4) * 4 + 2 + h, s // 2, part(256 * (s % 2), b)]

        def own_2y(rel, h, s):
            return A2[h, (y + rel) % 4, part(0, b)]

        def own_2x(rel, h, s):
            l, hi = x_of(rel)
            return B2[h, l * 2 + hi, part(0, b)]

        return (
            Ring(own_1x, 4, xp, xm, (r1x_s.at[b], c1x_s.at[b]), (r1x_r.at[b], c1x_r.at[b]), q1xs.at[b], q1xr.at[b]),
            Ring(own_1y, 4, yp, ym, (r1y_s.at[b], c1y_s.at[b]), (r1y_r.at[b], c1y_r.at[b]), q1ys.at[b], q1yr.at[b]),
            Ring(own_2x, 1, xp, xm, (r2x_s.at[b], c2x_s.at[b]), (r2x_r.at[b], c2x_r.at[b]), q2xs.at[b], q2xr.at[b]),
            Ring(own_2y, 1, yp, ym, (r2y_s.at[b], c2y_s.at[b]), (r2y_r.at[b], c2y_r.at[b]), q2ys.at[b], q2yr.at[b]),
        )

    every = [rings(0), rings(1)]

    def far(ring):
        ring.far(0)
        ring.far(1)

    def single(ring):
        ring.single(0)
        ring.single(1)

    def combine(ring):
        ring.combine(0)
        ring.combine(1)

    def zd_copy(k, b):
        return rcopy(Tb.at[k, part(0, b)], ZR.at[z, part(0, b)], zds.at[b, k], zdr.at[b, z], dev(x, y, 4 * c + k, c))

    def third(b):
        _, _, r2x, r2y = every[b]
        for h in range(2):
            r2y.mine_wait(h)
            T[h, part(0, b)] = r2y.mine(h, 0)
            r2x.mine_wait(h)
            T[2 + h, part(0, b)] = r2x.mine(h, 0)
        for k in range(4):
            @pl.when(4 * c + k != z)
            def _(k=k):
                Tb[k, part(0, b)] = T[k, part(0, b)].astype(BF16)
                zd_copy(k, b).start()

    owner = z // 4 == c

    def out_copy(i, b):
        to = (sib, far_same, far_other)[i]
        return rcopy(O.at[xh, b], O.at[xh, b], fs.at[b, i], fr.at[b, jnp.where(i == 0, 0, 1)], to)

    def fourth(b):
        @pl.when(owner)
        def _():
            for s in range(8):
                @pl.when(s != z)
                def _(s=s):
                    rcopy(Tb.at[0, part(0, b)], ZR.at[s, part(0, b)], zds.at[b, 0], zdr.at[b, s], sib).wait_recv()
            ZR[z, part(0, b)] = jnp.zeros((128, 128), BF16)
            tot = T[z % 4, part(0, b)]
            for s in range(8):
                tot = tot + ZR[s, part(0, b)].astype(F32)
            O[xh, b] = (tot / jnp.sqrt(F32(TOKENS))).T
            for i in range(3):
                out_copy(i, b).start()

    r1x, r1y, r2x, r2y = every[0]
    q1x, q1y, q2x, q2y = every[1]

    def step(i, u):
        product(i, u)
        return norm_both(i + AHEAD, u)

    lax.fori_loop(0, 2, step, 0)
    far(r1y)
    lax.fori_loop(2, 6, step, 0)
    r1x.far(0)
    z_serve(1, (0, 1, 2))
    lax.fori_loop(6, 10, step, 0)
    r1x.far(1)
    single(r1x)
    lax.fori_loop(10, 16, product, 0, unroll=2)
    single(r1y)
    z_serve(1, (3, 4, 5))
    combine(r1y)
    far(q1y)
    single(q1y)
    z_serve(1, (6, 7))
    combine(r1x)
    far(q1x)
    single(q1x)

    ACC[...] = jnp.zeros_like(ACC)

    def ng_chunk(yy, zz):
        j = yy * 8 + zz
        nt = (((1,), (1,)), ((), ()))
        ng = lax.dot_general(live_ref[:, 0:256], Wf[0, yy, zz].reshape(CH, 256), nt, preferred_element_type=F32)
        ng += lax.dot_general(live_ref[:, 256:512], Wf[1, yy, zz].reshape(CH, 256), nt, preferred_element_type=F32)
        NG[j] = ng
        v = X[j].astype(F32) * G[j] * ng
        ACC[...] += v[:, :128] + v[:, 128:]

    def ng_chunks(zz):
        lax.fori_loop(0, 4, lambda yy, u: (ng_chunk(yy, zz), u)[1], 0, unroll=True)

    def ng_step(k):
        for col in range(8):
            for d in range(2):
                share_in(col, d, k).wait_recv()
        for d in range(2 if k < 4 else 1):
            ng_chunks(z_at(d, k))

    def second(rings_b, b, along_y):
        r1x, r1y, r2x, r2y = rings_b
        one, two, to = (r1y, r2x, B2) if along_y else (r1x, r2y, A2)
        for h in range(2):
            one.mine_wait(h)
            for s in range(4):
                to[h, s, part(0, b)] = one.mine(h, s)
        far(two)
        single(two)

    combine(q1y)
    z_serve(2, (0, 1, 2))
    second(every[0], 0, True)
    combine(q1x)
    z_serve(2, (3, 4, 5))
    second(every[0], 0, False)
    combine(r2x)
    z_serve(2, (6, 7))
    combine(r2y)
    for col in range(8):
        share_own_in(col).wait_recv()
    ng_chunks(z)
    second(every[1], 1, True)
    second(every[1], 1, False)
    ng_step(1)
    third(0)
    z_serve(3, (0, 1, 2))
    combine(q2x)
    combine(q2y)
    ng_step(2)
    third(1)
    z_serve(3, (3, 4, 5))
    z_serve(3, (6, 7))
    fourth(0)
    ng_step(3)
    fourth(1)
    z_serve(4, range(8))
    ng_step(4)

    inner = jnp.sum(ACC[...], axis=1, keepdims=True)
    rb = RB[...]
    ACC[...] = rb * rb * rb * jnp.broadcast_to(inner, (TOK, 128)) / D

    def last(j, u):
        rb, co = RB[...], ACC[...]
        v = X[j].astype(F32)
        g = G[j]
        out = jnp.concatenate([rb, rb], axis=1) * g * NG[j] - v * jnp.concatenate([co, co], axis=1)
        X[j] = out.astype(BF16)
        return u

    lax.fori_loop(0, NCH, last, 0)

    for b in range(2):
        @pl.when(jnp.logical_not(owner))
        def _(b=b):
            rcopy(O.at[xh, b], O.at[xh, b], fs.at[b, 0], fr.at[b, 0], sib).wait_recv()

        rcopy(O.at[1 - xh, b], O.at[1 - xh, b], fs.at[b, 1], fr.at[b, 1], far_same).wait_recv()
        wg_ref[:, 128 * b : 128 * b + 128] = O[0, b]
        wg_ref[:, 256 + 128 * b : 384 + 128 * b] = O[1, b]

        @pl.when(owner)
        def _(b=b):
            for i in range(3):
                out_copy(i, b).wait_send()

        for k in range(4):
            @pl.when(4 * c + k != z)
            def _(k=k, b=b):
                zd_copy(k, b).wait_send()
        for ring in every[b]:
            ring.finish()
    for cp in ax_out:
        cp.wait_send()
    for col in range(2, 8):
        ay(col).wait_send()
    for col in range(8):
        for d in range(2):
            for k in range(1, 5):
                z_out(col, d, k).wait_send()
                share(col, d, k).wait_send()
    for col in range(8):
        share_own(col).wait_send()
    lt_copy.wait_send()
    lax.fori_loop(0, 16, lambda i, u: (n_copy(i).wait_send(), u)[1], 0)


def copy_out(ig, wg, ig_out, wg_out, sem):
    cps = [pltpu.make_async_copy(ig.at[j], ig_out.at[:, pl.ds(j * CH, CH)], sem.at[j]) for j in range(NCH)]
    cps.append(pltpu.make_async_copy(wg, wg_out, sem.at[NCH]))
    for cp in cps:
        cp.start()
    for cp in cps:
        cp.wait()


def on_device(layer_input, norm_gain, key_cotangent, segment_ids, key_weight):
    dma = pltpu.SemaphoreType.DMA
    vm = pltpu.VMEM

    def ring(subs, dtype=BF16):
        return [vm((2, 4, subs, 128, 128), dtype)] * 2

    def last(subs, dtype):
        return [vm((2, 2, subs, 128, 128), dtype)] * 2

    scratch = [
        vm((TOK, KW), BF16),
        vm((NCH, 1, CH), F32),
        vm((TOK, KW), BF16),
        vm((2, NY, NZ, 2, 128, 256), BF16),
        vm((16, 2 * TOK, CH), BF16),
        vm((16, TOK, CH), BF16),
        vm((KW, 2 * TOK), BF16),
        vm((16, 2, KW, 128), F32),
        vm((NCH, TOK, CH), F32),
        vm((TOK, 128), F32),
        vm((TOK, 128), F32),
        vm((2, 4, 256, 128), F32),
        vm((2, 4, 256, 128), F32),
        vm((4, 256, 128), F32),
        vm((4, 256, 128), BF16),
        vm((8, 256, 128), BF16),
        vm((2, 2, 128, 128), F32),
        *ring(4), *ring(4), *ring(1, F32), *ring(1, F32),
        *last(4, BF16), *last(4, BF16), *last(1, F32), *last(1, F32),
        dma((NCH,)), dma, dma, dma((16,)), dma((16,)), dma, dma,
        dma((2,)), dma((2,)), dma((6,)), dma((6,)),
        dma((8, 2, 4)), dma((8, 2, 4)), dma((8, 2, 4)), dma((8, 2, 4)), dma((8,)), dma((8,)),
        *[dma((2, 6))] * 8,
        dma((2, 4)), dma((2, 8)), dma((2, 3)), dma((2, 2)),
    ]
    anyspace = pl.BlockSpec(memory_space=pl.ANY)
    vspace = pl.BlockSpec(memory_space=pltpu.VMEM)
    wg, ig = pl.pallas_call(
        kernel,
        name="key_projection_backward",
        out_shape=(pltpu.VMEM((128, KW), F32), pltpu.VMEM((NCH, TOK, CH), BF16)),
        in_specs=[anyspace, vspace, anyspace, vspace, anyspace],
        out_specs=(vspace, vspace),
        scratch_shapes=scratch,
        compiler_params=pltpu.CompilerParams(
            collective_id=0, has_side_effects=True, vmem_limit_bytes=53 * 2**20
        ),
    )(layer_input, norm_gain, key_cotangent, segment_ids, key_weight)
    ig, wg = pl.pallas_call(
        copy_out,
        name="copy_out",
        out_shape=(jax.ShapeDtypeStruct((TOK, D), BF16), jax.ShapeDtypeStruct((128, KW), F32)),
        in_specs=[vspace] * 2,
        out_specs=(anyspace,) * 2,
        scratch_shapes=[dma((NCH + 1,))],
        compiler_params=pltpu.CompilerParams(vmem_limit_bytes=2**20),
    )(pltpu.with_memory_space_constraint(ig, pltpu.VMEM), pltpu.with_memory_space_constraint(wg, pltpu.VMEM))
    return wg, ig


def solution(mesh):
    placed = (
        P(("blk", "rep"), None),
        P(),
        P(("blk", "rep"), None),
        P(("blk", "rep")),
        P("blk", None),
    )
    return jax.shard_map(
        on_device,
        mesh=mesh,
        in_specs=placed,
        out_specs=(P("blk", None), P(("blk", "rep"), None)),
        check_vma=False,
    )
```
